512 devices in a mesh: dp: 512 (over x, z, y, core).
Axes of the slice: x: 4, y: 4, z: 16, core: 2. Of those that a mesh axis runs over, the one named last changes fastest.
Arguments:
- image_emb: bfloat16 [262144, 1152], P('dp'), may hold values from -0.71875 to 0.71875
- text_emb: bfloat16 [262144, 1152], P('dp'), may hold values from -0.71875 to 0.71875
- logit_scale: float32 [1], replicated, may hold values from 2 to 8
- logit_bias: float32 [1], replicated, may hold values from -3 to 0
Outputs:
- image_grad: bfloat16 [262144, 1152], P('dp')
- text_grad: bfloat16 [262144, 1152], P('dp')
- loss_rows: float32 [262144], P('dp')
The draws below stay inside these ranges and needn't reach their ends.
All inputs are finite; a program needn't handle non-finite values.
Results may differ from the reference program's by a relative error of at most 0.005.
Values may be sent and summed in bfloat16 or wider, within the bound.
A program may use at most 64 MiB of HBM per device.

```python
import math
import jax
import jax.numpy as jnp
from jax import lax

D = 1152
ROWS = 512
BATCH = 262144
N_DP = 512


def level_of(own_key, shape, cuts, smallest, high):
    loudness = 1.0
    for dim, parts in cuts:
        steps = jax.random.uniform(jax.random.fold_in(jax.random.fold_in(own_key, 6), dim), (parts,), jnp.float32, smallest / len(cuts), high / len(cuts))
        loudness = loudness * jnp.repeat(jnp.exp(steps), shape[dim] // parts).reshape((-1,) + (1,) * (len(shape) - 1 - dim))
    return loudness


def centred(stream_key, dims, deviation, bound, pieces=(), held_as=jnp.bfloat16):
    entries = deviation * jax.random.normal(stream_key, dims, jnp.float32)
    if pieces:
        entries = entries * level_of(stream_key, dims, pieces, -0.22, 0.18)
    return jnp.clip(entries, -bound, bound).astype(held_as)


def setup_inputs(seed: int = 0) -> dict:
    seeds = jax.random.split(jax.random.key(seed), 5)
    return {
        "image_emb": centred(seeds[0], (BATCH, D), 0.12, 0.71875, ((0, 512),)),
        "text_emb": centred(seeds[1], (BATCH, D), 0.12, 0.71875, ((0, 512),)),
        "logit_scale": jnp.clip(jnp.exp(jax.random.uniform(seeds[2], (1,), jnp.float32, math.log(2.0), math.log(8.0))), 2.0, 8.0),
        "logit_bias": jnp.clip(jax.random.uniform(seeds[3], (1,), jnp.float32, -3.0, 0.0), -3.0, 0.0),
    }


def block_terms(images, texts, scale, bias, positive):
    logits = jnp.dot(images, texts.T, preferred_element_type=jnp.float32) * scale + bias
    count = logits.shape[0]
    rowpos = lax.broadcasted_iota(jnp.int32, (count, count), 0)
    colpos = lax.broadcasted_iota(jnp.int32, (count, count), 1)
    labels = (rowpos == colpos).astype(jnp.float32) * positive
    losses = jax.nn.softplus(logits) - labels * logits
    weights = ((jax.nn.sigmoid(logits) - labels) * scale).astype(jnp.bfloat16)
    return jnp.sum(losses, axis=1), weights


def reference(image_emb, text_emb, logit_scale, logit_bias):
    images = image_emb.reshape(N_DP, ROWS, D)
    texts = text_emb.reshape(N_DP, ROWS, D)
    back_one = jnp.roll(texts, 1, axis=0)
    back_two = jnp.roll(texts, 2, axis=0)
    scale = logit_scale[0]
    bias = logit_bias[0]

    def one_device(items):
        img, own, first, second = items
        loss_a, weight_a = block_terms(img, own, scale, bias, 1.0)
        loss_b, weight_b = block_terms(img, first, scale, bias, 0.0)
        loss_c, weight_c = block_terms(img, second, scale, bias, 0.0)
        grad_img = jnp.dot(weight_a, own, preferred_element_type=jnp.float32)
        grad_img = grad_img + jnp.dot(weight_b, first, preferred_element_type=jnp.float32)
        grad_img = grad_img + jnp.dot(weight_c, second, preferred_element_type=jnp.float32)
        part_a = jnp.dot(weight_a.T, img, preferred_element_type=jnp.float32)
        part_b = jnp.dot(weight_b.T, img, preferred_element_type=jnp.float32).astype(jnp.bfloat16)
        part_c = jnp.dot(weight_c.T, img, preferred_element_type=jnp.float32).astype(jnp.bfloat16)
        losses = (loss_a + loss_b + loss_c) / (3.0 * ROWS)
        return grad_img.astype(jnp.bfloat16), part_a, part_b, part_c, losses

    grad_img, part_a, part_b, part_c, losses = lax.map(one_device, (images, texts, back_one, back_two))
    total = part_a + jnp.roll(part_b.astype(jnp.float32), -1, axis=0) + jnp.roll(part_c.astype(jnp.float32), -2, axis=0)
    return grad_img.reshape(BATCH, D), total.astype(jnp.bfloat16).reshape(BATCH, D), losses.reshape(BATCH)
```

```python
import jax
import jax.numpy as jnp
from jax import lax
from jax.experimental import pallas as pl
from jax.experimental.pallas import tpu as pltpu
from jax.sharding import PartitionSpec as P

MESH = pl.DeviceIdType.MESH
CHUNKS = 4


def exchange_kernel(
    count,
    scale_ref,
    bias_ref,
    image_ref,
    text_ref,
    grad_ref,
    loss_ref,
    own,
    early,
    first,
    second,
    passed,
    total,
    logs,
    lins,
    own_sem,
    early_sem,
    first_sem,
    second_sem,
    passed_sem,
    ready_sem,
):
    rows, depth = image_ref.shape
    step = rows // CHUNKS
    me = lax.axis_index("dp")
    odd = lax.rem(me, 2)
    even = 1 - odd
    other = me + 1 - 2 * odd
    ahead = lax.rem(me + 2, count)
    behind = lax.rem(me + count - 2, count)

    barrier = pltpu.get_barrier_semaphore()
    for device in (behind, other):
        pl.semaphore_signal(barrier, inc=1, device_id=(device,), device_id_type=MESH)

    loads = []
    for place, ref in ((0, image_ref), (1, text_ref)):
        load = pltpu.make_async_copy(ref, own.at[place], own_sem.at[place])
        load.start()
        loads.append(load)

    def part(index):
        return pl.ds(index * step, step)

    def send(source, target, sems, index, device):
        return pltpu.make_async_remote_copy(
            src_ref=source.at[part(index)],
            dst_ref=target.at[part(index)],
            send_sem=sems.at[0, index],
            recv_sem=sems.at[1, index],
            device_id=(device,),
            device_id_type=MESH,
        )

    texts_first = [send(own.at[1], first, first_sem, c, ahead) for c in range(CHUNKS)]
    texts_second = [send(own.at[1], second, second_sem, c, ahead) for c in range(CHUNKS)]
    images_first = [send(own.at[0], first, first_sem, c, behind) for c in range(CHUNKS)]
    images_second = [send(own.at[0], second, second_sem, c, behind) for c in range(CHUNKS)]
    to_other = pltpu.make_async_remote_copy(
        src_ref=own.at[even],
        dst_ref=early,
        send_sem=early_sem.at[0],
        recv_sem=early_sem.at[1],
        device_id=(other,),
        device_id_type=MESH,
    )
    onward = [send(first, passed, passed_sem, c, other) for c in range(CHUNKS)]

    total[...] = jnp.zeros_like(total)
    logs[...] = jnp.zeros_like(logs)
    lins[...] = jnp.zeros_like(lins)
    for load in loads:
        load.wait()
    pl.semaphore_wait(barrier, 2)
    pl.semaphore_signal(ready_sem, inc=1, device_id=(ahead,), device_id_type=MESH)

    @pl.when(odd == 1)
    def _():
        for copy in texts_first:
            copy.start()

    @pl.when(odd == 0)
    def _():
        for copy in texts_second:
            copy.start()

    to_other.start()
    pl.semaphore_wait(ready_sem, 1)

    @pl.when(odd == 1)
    def _():
        for copy in images_second:
            copy.start()

    @pl.when(odd == 0)
    def _():
        for copy in images_first:
            copy.start()

    scale = scale_ref[0]
    bias = bias_ref[0]

    def weigh(side, block, base=None):
        logits = (
            lax.dot_general(
                own[side], block, (((1,), (1,)), ((), ())), preferred_element_type=jnp.float32
            )
            * scale
            + bias
        )
        small = jnp.exp(-jnp.abs(logits))
        below = 1.0 + small
        positive = logits >= 0.0
        sigmoid = jnp.where(positive, 1.0, small) / below
        linear = jnp.maximum(logits, 0.0)
        if base is not None:
            row = lax.broadcasted_iota(jnp.int32, logits.shape, 0)
            column = lax.broadcasted_iota(jnp.int32, logits.shape, 1) + base
            label = row == column
            linear = jnp.where(label, linear - logits, linear)
            sigmoid = jnp.where(label, sigmoid - 1.0, sigmoid)
        for lane in range(0, logits.shape[1], 128):
            here = slice(lane, lane + 128)
            logs[side] = logs[side] * below[:, here] + small[:, here]
            lins[side] += linear[:, here]
        return (sigmoid * scale).astype(jnp.bfloat16)

    def add(side, block):
        weights = weigh(side, block)
        total[side] += jnp.dot(weights, block, preferred_element_type=jnp.float32)

    for c in range(CHUNKS):
        block = own[1, part(c)]
        weights = weigh(0, block, c * step)
        total[0] += jnp.dot(weights, block, preferred_element_type=jnp.float32)
        total[1, part(c)] += lax.dot_general(
            weights, own[0], (((0,), (0,)), ((), ())), preferred_element_type=jnp.float32
        )

    to_other.wait_recv()
    for c in range(CHUNKS):
        add(even, early[part(c)])

    for c in range(CHUNKS):
        onward_in = onward[c]
        texts_first[c].wait_recv()
        onward[c].start()
        add(even, first[part(c)])
        texts_second[c].wait_recv()
        add(odd, second[part(c)])
        onward[c].wait_recv()
        add(odd, passed[part(c)])

    grad_ref[...] = total[...].astype(jnp.bfloat16)
    loss_ref[...] = lins[0] + jnp.log1p(logs[0])

    to_other.wait_send()
    for c in range(CHUNKS):
        texts_first[c].wait_send()
        texts_second[c].wait_send()
        onward[c].wait_send()


def per_device(count, image_emb, text_emb, logit_scale, logit_bias):
    rows, depth = image_emb.shape
    block = pltpu.VMEM((rows, depth), jnp.bfloat16)
    pair = pltpu.SemaphoreType.DMA((2, CHUNKS))
    grads, losses = pl.pallas_call(
        lambda *refs: exchange_kernel(count, *refs),
        out_shape=(
            jax.ShapeDtypeStruct((2, rows, depth), jnp.bfloat16),
            jax.ShapeDtypeStruct((rows, 128), jnp.float32),
        ),
        in_specs=[pl.BlockSpec(memory_space=pltpu.SMEM)] * 2
        + [pl.BlockSpec(memory_space=pl.ANY)] * 2,
        out_specs=[pl.BlockSpec(memory_space=pltpu.VMEM)] * 2,
        scratch_shapes=[
            pltpu.VMEM((2, rows, depth), jnp.bfloat16),
            block,
            block,
            block,
            block,
            pltpu.VMEM((2, rows, depth), jnp.float32),
            pltpu.VMEM((2, rows, 128), jnp.float32),
            pltpu.VMEM((2, rows, 128), jnp.float32),
            pltpu.SemaphoreType.DMA((2,)),
            pltpu.SemaphoreType.DMA((2,)),
            pair,
            pair,
            pair,
            pltpu.SemaphoreType.REGULAR,
        ],
        compiler_params=pltpu.CompilerParams(
            collective_id=0, has_side_effects=True, vmem_limit_bytes=56 << 20
        ),
        cost_estimate=pl.CostEstimate(
            flops=22 * rows * rows * depth, bytes_accessed=8 * rows * depth, transcendentals=0
        ),
    )(logit_scale, logit_bias, image_emb, text_emb)
    loss_rows = jnp.sum(losses, axis=1) / (3.0 * rows)
    return grads[0], grads[1], loss_rows


def solution(mesh):
    count = mesh.shape["dp"]
    in_specs = (P("dp", None), P("dp", None), P(), P())
    out_specs = (P("dp", None), P("dp", None), P("dp"))
    return jax.shard_map(
        lambda *arrays: per_device(count, *arrays),
        mesh=mesh,
        in_specs=in_specs,
        out_specs=out_specs,
        check_vma=False,
    )
```

```python
import jax
import jax.numpy as jnp
from jax import lax
from jax.experimental import pallas as pl
from jax.experimental.pallas import tpu as pltpu
from jax.sharding import PartitionSpec as P

MESH = pl.DeviceIdType.MESH
WIDE, NARROW, TAIL = 128, 64, 2
PIECES = 16
LOG2E = 1.4426950408889634


def exchange_kernel(
    count,
    scale_ref,
    bias_ref,
    image_ref,
    text_ref,
    total,
    logs,
    lins,
    own,
    early,
    first,
    late,
    own_sem,
    early_sem,
    first_sem,
    second_sem,
    passed_sem,
    ready_sem,
):
    rows, depth = image_ref.shape
    wide = (rows - NARROW * TAIL) // WIDE
    me = lax.axis_index("dp")
    odd = lax.rem(me, 2)
    even = 1 - odd
    other = me + 1 - 2 * odd
    ahead = lax.rem(me + 2, count)
    behind = lax.rem(me + count - 2, count)

    barrier = pltpu.get_barrier_semaphore()
    for device in (behind, other):
        pl.semaphore_signal(barrier, inc=1, device_id=(device,), device_id_type=MESH)

    loads = []
    for place, ref in ((0, image_ref), (1, text_ref)):
        load = pltpu.make_async_copy(ref, own.at[place], own_sem.at[place])
        load.start()
        loads.append(load)

    def span(index, narrow):
        if narrow:
            start = wide * WIDE + index * NARROW
            return pl.ds(start, NARROW), wide + index
        return pl.ds(pl.multiple_of(index * WIDE, WIDE), WIDE), index

    def send(source, target, sems, where, device, place=None):
        here, index = where
        there = here
        if place is not None:
            there = pl.ds(2 * here.start + place * here.size, here.size)
        return pltpu.make_async_remote_copy(
            src_ref=source.at[here],
            dst_ref=target.at[there],
            send_sem=sems.at[0, index],
            recv_sem=sems.at[1, index],
            device_id=(device,),
            device_id_type=MESH,
        )

    pieces = [span(c, False) for c in range(wide)] + [span(c, True) for c in range(TAIL)]

    def start_all(source, target, sems, device, place=None):
        for where in pieces:
            send(source, target, sems, where, device, place).start()

    to_other = pltpu.make_async_remote_copy(
        src_ref=own.at[even],
        dst_ref=early,
        send_sem=early_sem.at[0],
        recv_sem=early_sem.at[1],
        device_id=(other,),
        device_id_type=MESH,
    )

    total[...] = jnp.zeros_like(total)
    logs[...] = jnp.zeros_like(logs)
    lins[...] = jnp.zeros_like(lins)
    for load in loads:
        load.wait()
    pl.semaphore_wait(barrier, 2)

    @pl.when(odd == 1)
    def _():
        start_all(own.at[1], first, first_sem, ahead)

    pl.semaphore_signal(ready_sem, inc=1, device_id=(ahead,), device_id_type=MESH)
    to_other.start()

    @pl.when(odd == 0)
    def _():
        pl.semaphore_wait(ready_sem, 1)
        start_all(own.at[0], first, first_sem, behind)

    scale = scale_ref[0]
    slope = scale * LOG2E
    shift = bias_ref[0] * LOG2E

    halves = [pl.ds(0, rows // 2), pl.ds(rows // 2, rows // 2)]

    def weigh(side, half, block, base=None):
        logits = (
            lax.dot_general(
                own[side, half], block, (((1,), (1,)), ((), ())), preferred_element_type=jnp.float32
            )
            * slope
            + shift
        )
        small = jnp.exp2(jnp.minimum(logits, -logits))
        below = 1.0 + small
        positive = logits >= 0.0
        linear = jnp.maximum(logits, 0.0)
        if base is None:
            weights = jnp.where(positive, scale, scale * small)
        else:
            row = lax.broadcasted_iota(jnp.int32, logits.shape, 0) + half.start
            column = lax.broadcasted_iota(jnp.int32, logits.shape, 1) + base
            label = row == column
            linear = jnp.where(label, linear - logits, linear)
            weights = jnp.where(
                label,
                jnp.where(positive, -scale * small, -scale),
                jnp.where(positive, scale, scale * small),
            )
        width = min(logits.shape[1], 128)
        for lane in range(0, logits.shape[1], width):
            here = slice(lane, lane + width)
            logs[side, half, :width] = logs[side, half, :width] * below[:, here] + small[:, here]
            lins[side, half, :width] += linear[:, here]
        return (weights * pltpu.reciprocal(below, approx=True)).astype(jnp.bfloat16)

    def add(side, block):
        weights = [weigh(side, half, block) for half in halves]
        for half, factor in zip(halves, weights):
            total[side, half] += jnp.dot(factor, block, preferred_element_type=jnp.float32)

    @pl.loop(0, rows // 256)
    def _(c):
        here = pl.ds(pl.multiple_of(c * 256, 256), 256)
        block = own[1, here]
        weights = [weigh(0, half, block, c * 256) for half in halves]
        for half, factor in zip(halves, weights):
            total[0, half] += jnp.dot(factor, block, preferred_element_type=jnp.float32)
        total[1, here] += sum(
            lax.dot_general(
                factor, own[0, half], (((0,), (0,)), ((), ())), preferred_element_type=jnp.float32
            )
            for half, factor in zip(halves, weights)
        )

    send(own.at[odd], first, first_sem, pieces[0], other).wait_send()

    @pl.when(odd == 1)
    def _():
        pl.semaphore_wait(ready_sem, 1)
        start_all(own.at[0], late, second_sem, behind, 0)

    @pl.when(odd == 0)
    def _():
        start_all(own.at[1], late, second_sem, ahead, 0)

    to_other.wait_recv()

    @pl.loop(0, rows // 256)
    def _(c):
        add(even, early[pl.ds(pl.multiple_of(c * 256, 256), 256)])

    def turn(index, narrow):
        where = span(index, narrow)
        here = where[0]
        onward = send(first, late, passed_sem, where, other, 1)
        send(first, first, first_sem, where, other).wait_recv()
        onward.start()
        add(even, first[here])
        onward.wait_recv()
        send(own.at[0], late, second_sem, where, other, 0).wait_recv()
        add(odd, late[pl.ds(2 * here.start, 2 * here.size)])

    pl.loop(0, wide)(lambda c: turn(c, False))
    for c in range(TAIL):
        turn(c, True)

    to_other.wait_send()
    for where in pieces[1:]:
        send(own.at[0], first, first_sem, where, other).wait_send()
    for where in pieces:
        send(own.at[0], late, second_sem, where, other, 0).wait_send()
        send(first, late, passed_sem, where, other, 1).wait_send()


def finish_kernel(total, logs, lins, image_out, text_out, loss_out, held, loss, sems, loss_sem):
    rows = held.shape[1]
    step = rows // PIECES
    copies = []
    for place, out in ((0, image_out), (1, text_out)):
        for c in range(PIECES):
            here = pl.ds(c * step, step)
            held[place, here] = total[place, here].astype(jnp.bfloat16)
            copy = pltpu.make_async_copy(held.at[place, here], out.at[here], sems.at[place, c])
            copy.start()
            copies.append(copy)
    sums = lins[0] * (1.0 / LOG2E) + jnp.log1p(logs[0])
    loss[...] = jnp.sum(sums.T, axis=0) / (3.0 * rows)
    last = pltpu.make_async_copy(loss, loss_out, loss_sem)
    last.start()
    for copy in copies:
        copy.wait()
    last.wait()


def per_device(count, image_emb, text_emb, logit_scale, logit_bias):
    rows, depth = image_emb.shape
    inputs = [pltpu.with_memory_space_constraint(x, pltpu.HBM) for x in (image_emb, text_emb)]
    block = pltpu.VMEM((rows, depth), jnp.bfloat16)
    pieces = (rows - NARROW * TAIL) // WIDE + TAIL
    pair = pltpu.SemaphoreType.DMA((2, pieces))
    totals = pl.pallas_call(
        lambda *refs: exchange_kernel(count, *refs),
        out_shape=(
            pltpu.VMEM((2, rows, depth), jnp.float32),
            pltpu.VMEM((2, rows, 128), jnp.float32),
            pltpu.VMEM((2, rows, 128), jnp.float32),
        ),
        in_specs=[pl.BlockSpec(memory_space=pltpu.SMEM)] * 2
        + [pl.BlockSpec(memory_space=pltpu.HBM)] * 2,
        out_specs=[pl.BlockSpec(memory_space=pltpu.VMEM)] * 3,
        scratch_shapes=[
            pltpu.VMEM((2, rows, depth), jnp.bfloat16),
            block,
            block,
            pltpu.VMEM((2 * rows, depth), jnp.bfloat16),
            pltpu.SemaphoreType.DMA((2,)),
            pltpu.SemaphoreType.DMA((2,)),
            pair,
            pair,
            pair,
            pltpu.SemaphoreType.REGULAR,
        ],
        compiler_params=pltpu.CompilerParams(
            collective_id=0, has_side_effects=True, vmem_limit_bytes=40 << 20
        ),
        cost_estimate=pl.CostEstimate(
            flops=22 * rows * rows * depth, bytes_accessed=8 * rows * depth, transcendentals=0
        ),
    )(logit_scale, logit_bias, *inputs)
    return pl.pallas_call(
        finish_kernel,
        out_shape=(
            jax.ShapeDtypeStruct((rows, depth), jnp.bfloat16),
            jax.ShapeDtypeStruct((rows, depth), jnp.bfloat16),
            jax.ShapeDtypeStruct((rows,), jnp.float32),
        ),
        in_specs=[pl.BlockSpec(memory_space=pltpu.VMEM)] * 3,
        out_specs=[pl.BlockSpec(memory_space=pl.ANY)] * 3,
        scratch_shapes=[
            pltpu.VMEM((2, rows, depth), jnp.bfloat16),
            pltpu.VMEM((rows,), jnp.float32),
            pltpu.SemaphoreType.DMA((2, PIECES)),
            pltpu.SemaphoreType.DMA,
        ],
        compiler_params=pltpu.CompilerParams(vmem_limit_bytes=16 << 20),
    )(*totals)


def solution(mesh):
    count = mesh.shape["dp"]
    in_specs = (P("dp", None), P("dp", None), P(), P())
    out_specs = (P("dp", None), P("dp", None), P("dp"))
    return jax.shard_map(
        lambda *arrays: per_device(count, *arrays),
        mesh=mesh,
        in_specs=in_specs,
        out_specs=out_specs,
        check_vma=False,
    )
```

```python
import jax
import jax.numpy as jnp
from jax import lax
from jax.experimental import pallas as pl
from jax.experimental.pallas import tpu as pltpu
from jax.sharding import PartitionSpec as P

MESH = pl.DeviceIdType.MESH
WIDE, NARROW, TAIL = 128, 64, 2
PIECES = 16
PLANE = 128
RELAYS = ((0, 104), (1, 112))
HEAD_START = 1
LOG2E = 1.4426950408889634


def exchange_kernel(
    count,
    scale_ref,
    bias_ref,
    image_ref,
    text_ref,
    total,
    logs,
    lins,
    own,
    early,
    first,
    relayed,
    late,
    own_sem,
    early_sem,
    first_sem,
    second_sem,
    passed_sem,
    relay_sem,
    ready_sem,
    other_sem,
):
    rows, depth = image_ref.shape
    wide = (rows - NARROW * TAIL) // WIDE
    me = lax.axis_index("dp")
    odd = lax.rem(me, 2)
    even = 1 - odd
    other = me + 1 - 2 * odd
    ahead = lax.rem(me + 2, count)
    behind = lax.rem(me + count - 2, count)

    place = lax.rem(me, PLANE)
    is_head = place < 2
    is_tail = place >= PLANE - 2
    even_head = place == 0
    even_tail = place == PLANE - 2
    is_relay = [place == there for _, there in RELAYS]

    def tell(semaphore, device):
        pl.semaphore_signal(semaphore, inc=1, device_id=(device,), device_id_type=MESH)

    barrier = pltpu.get_barrier_semaphore()
    tell(barrier, behind)

    @pl.when(odd == 1)
    def _():
        tell(barrier, other)

    @pl.when(even_head)
    def _():
        for _, there in RELAYS:
            tell(barrier, lax.rem(me - PLANE + there + count, count))

    for chosen, (_, there) in zip(is_relay, RELAYS):

        @pl.when(chosen)
        def _(there=there):
            tell(barrier, me - there + PLANE - 2)

    heard = 1 + even + jnp.where(even_tail, len(RELAYS), 0)
    heard += sum(jnp.where(chosen, 1, 0) for chosen in is_relay)

    loads = []
    for side, ref in ((0, image_ref), (1, text_ref)):
        load = pltpu.make_async_copy(ref, own.at[side], own_sem.at[side])
        load.start()
        loads.append(load)

    def span(index, narrow):
        if narrow:
            start = wide * WIDE + index * NARROW
            return pl.ds(start, NARROW), wide + index
        start = index * WIDE
        if not isinstance(index, int):
            start = pl.multiple_of(start, WIDE)
        return pl.ds(start, WIDE), index

    def send(source, target, sems, where, device, place=None):
        here, index = where
        there = here
        if place is not None:
            there = pl.ds(2 * here.start + place * here.size, here.size)
        return pltpu.make_async_remote_copy(
            src_ref=source.at[here],
            dst_ref=target.at[there],
            send_sem=sems.at[0, index],
            recv_sem=sems.at[1, index],
            device_id=(device,),
            device_id_type=MESH,
        )

    pieces = [span(c, False) for c in range(wide)] + [span(c, True) for c in range(TAIL)]

    def start_all(source, target, sems, device, place=None):
        for where in pieces:
            send(source, target, sems, where, device, place).start()

    def to_relay(piece, there):
        here, index = pieces[piece]
        return pltpu.make_async_remote_copy(
            src_ref=text_ref.at[here],
            dst_ref=relayed.at[pl.ds(0, here.size)],
            send_sem=second_sem.at[0, index],
            recv_sem=relay_sem.at[1],
            device_id=(me - (PLANE - 2) + there,),
            device_id_type=MESH,
        )

    def from_relay(piece, there):
        here, index = pieces[piece]
        return pltpu.make_async_remote_copy(
            src_ref=relayed.at[pl.ds(0, here.size)],
            dst_ref=late.at[pl.ds(2 * here.start, here.size)],
            send_sem=relay_sem.at[0],
            recv_sem=second_sem.at[1, index],
            device_id=(lax.rem(me - there + PLANE, count),),
            device_id_type=MESH,
        )

    to_other = pltpu.make_async_remote_copy(
        src_ref=own.at[even],
        dst_ref=early,
        send_sem=early_sem.at[0],
        recv_sem=early_sem.at[1],
        device_id=(other,),
        device_id_type=MESH,
    )

    pl.semaphore_wait(barrier, heard)
    tell(ready_sem, ahead)

    neither = jnp.logical_and(place > 0, place < PLANE - 2)
    early_ready = jnp.logical_not(is_head)

    @pl.when(odd == 1)
    def _():
        start_all(text_ref, first, first_sem, ahead)

    @pl.when(even_head)
    def _():
        start_all(text_ref, late, second_sem, ahead, 0)

    @pl.when(even_tail)
    def _():
        for piece, there in RELAYS:
            to_relay(piece, there).start()

    @pl.when(odd == 0)
    def _():
        tell(other_sem, other)

    total[...] = jnp.zeros_like(total)
    logs[...] = jnp.zeros_like(logs)
    lins[...] = jnp.zeros_like(lins)

    @pl.when(jnp.logical_and(even == 1, early_ready))
    def _():
        pl.semaphore_wait(ready_sem, 1)
        start_all(image_ref, first, first_sem, behind)

    for load in loads:
        load.wait()

    @pl.when(odd == 1)
    def _():
        pl.semaphore_wait(other_sem, 1)

    to_other.start()

    scale = scale_ref[0]
    slope = scale * LOG2E
    shift = bias_ref[0] * LOG2E

    halves = [pl.ds(0, rows // 2), pl.ds(rows // 2, rows // 2)]

    def weigh(side, half, block, base=None):
        logits = (
            lax.dot_general(
                own[side, half], block, (((1,), (1,)), ((), ())), preferred_element_type=jnp.float32
            )
            * slope
            + shift
        )
        small = jnp.exp2(jnp.minimum(logits, -logits))
        below = 1.0 + small
        positive = logits >= 0.0
        linear = jnp.maximum(logits, 0.0)
        if base is None:
            weights = jnp.where(positive, scale, scale * small)
        else:
            row = lax.broadcasted_iota(jnp.int32, logits.shape, 0) + half.start
            column = lax.broadcasted_iota(jnp.int32, logits.shape, 1) + base
            label = row == column
            linear = jnp.where(label, linear - logits, linear)
            weights = jnp.where(
                label,
                jnp.where(positive, -scale * small, -scale),
                jnp.where(positive, scale, scale * small),
            )
        width = min(logits.shape[1], 128)
        for lane in range(0, logits.shape[1], width):
            here = slice(lane, lane + width)
            logs[side, half, :width] = logs[side, half, :width] * below[:, here] + small[:, here]
            lins[side, half, :width] += linear[:, here]
        return (weights * pltpu.reciprocal(below, approx=True)).astype(jnp.bfloat16)

    def add(side, block):
        weights = [weigh(side, half, block) for half in halves]
        for half, factor in zip(halves, weights):
            total[side, half] += jnp.dot(factor, block, preferred_element_type=jnp.float32)

    @pl.loop(0, rows // 256)
    def _(c):
        here = pl.ds(pl.multiple_of(c * 256, 256), 256)
        block = own[1, here]
        weights = [weigh(0, half, block, c * 256) for half in halves]
        for half, factor in zip(halves, weights):
            total[0, half] += jnp.dot(factor, block, preferred_element_type=jnp.float32)
        total[1, here] += sum(
            lax.dot_general(
                factor, own[0, half], (((0,), (0,)), ((), ())), preferred_element_type=jnp.float32
            )
            for half, factor in zip(halves, weights)
        )

    started = jnp.logical_or(odd == 1, early_ready)

    @pl.when(started)
    def _():
        send(own.at[odd], first, first_sem, pieces[0], other).wait_send()

    @pl.when(jnp.logical_and(odd == 1, early_ready))
    def _():
        pl.semaphore_wait(ready_sem, 1)
        start_all(image_ref, late, second_sem, behind, 0)

    @pl.when(jnp.logical_and(even == 1, neither))
    def _():
        start_all(text_ref, late, second_sem, ahead, 0)

    for chosen, (piece, there) in zip(is_relay, RELAYS):

        @pl.when(chosen)
        def _(piece=piece, there=there):
            to_relay(piece, there).wait_recv()
            from_relay(piece, there).start()

    to_other.wait_recv()

    @pl.loop(0, rows // 256)
    def _(c):
        add(even, early[pl.ds(pl.multiple_of(c * 256, 256), 256)])

    @pl.when(even_tail)
    def _():
        for piece, where in enumerate(pieces):
            if piece not in [index for index, _ in RELAYS]:
                send(text_ref, late, second_sem, where, ahead, 0).start()

    @pl.when(is_head)
    def _():
        pl.semaphore_wait(ready_sem, 1)

        @pl.when(odd == 1)
        def _():
            start_all(image_ref, late, second_sem, behind, 0)

        @pl.when(odd == 0)
        def _():
            @pl.when(me != 0)
            def _():
                start_all(image_ref, first, first_sem, behind)

            for index, where in enumerate(pieces):
                send(first, first, first_sem, where, other).wait_recv()
                send(first, late, passed_sem, where, other, 1).start()
                if index == HEAD_START:

                    @pl.when(me == 0)
                    def _():
                        start_all(image_ref, first, first_sem, behind)

    def turn(index, narrow):
        where = span(index, narrow)
        here = where[0]
        onward = send(first, late, passed_sem, where, other, 1)

        @pl.when(jnp.logical_not(even_head))
        def _():
            send(first, first, first_sem, where, other).wait_recv()
            onward.start()

        add(even, first[here])
        onward.wait_recv()
        send(own.at[0], late, second_sem, where, other, 0).wait_recv()
        add(odd, late[pl.ds(2 * here.start, 2 * here.size)])

    @pl.loop(0, wide)
    def _(c):
        turn(c, False)
    for c in range(TAIL):
        turn(c, True)

    to_other.wait_send()

    @pl.when(jnp.logical_not(started))
    def _():
        send(own.at[0], first, first_sem, pieces[0], other).wait_send()

    for chosen, (piece, there) in zip(is_relay, RELAYS):

        @pl.when(chosen)
        def _(piece=piece, there=there):
            from_relay(piece, there).wait_send()

    for where in pieces[1:]:
        send(own.at[0], first, first_sem, where, other).wait_send()
    for where in pieces:
        send(own.at[0], late, second_sem, where, other, 0).wait_send()
        send(first, late, passed_sem, where, other, 1).wait_send()


def finish_kernel(total, logs, lins, image_out, text_out, loss_out, held, loss, sems, loss_sem):
    rows = held.shape[1]
    step = rows // PIECES
    copies = []
    for place, out in ((0, image_out), (1, text_out)):
        for c in range(PIECES):
            here = pl.ds(c * step, step)
            held[place, here] = total[place, here].astype(jnp.bfloat16)
            copy = pltpu.make_async_copy(held.at[place, here], out.at[here], sems.at[place, c])
            copy.start()
            copies.append(copy)
    sums = lins[0] * (1.0 / LOG2E) + jnp.log1p(logs[0])
    loss[...] = jnp.sum(sums.T, axis=0) / (3.0 * rows)
    last = pltpu.make_async_copy(loss, loss_out, loss_sem)
    last.start()
    for copy in copies:
        copy.wait()
    last.wait()


def per_device(count, image_emb, text_emb, logit_scale, logit_bias):
    rows, depth = image_emb.shape
    inputs = [pltpu.with_memory_space_constraint(x, pltpu.HBM) for x in (image_emb, text_emb)]
    block = pltpu.VMEM((rows, depth), jnp.bfloat16)
    pieces = (rows - NARROW * TAIL) // WIDE + TAIL
    pair = pltpu.SemaphoreType.DMA((2, pieces))
    totals = pl.pallas_call(
        lambda *refs: exchange_kernel(count, *refs),
        out_shape=(
            pltpu.VMEM((2, rows, depth), jnp.float32),
            pltpu.VMEM((2, rows, 128), jnp.float32),
            pltpu.VMEM((2, rows, 128), jnp.float32),
        ),
        in_specs=[pl.BlockSpec(memory_space=pltpu.SMEM)] * 2
        + [pl.BlockSpec(memory_space=pltpu.HBM)] * 2,
        out_specs=[pl.BlockSpec(memory_space=pltpu.VMEM)] * 3,
        scratch_shapes=[
            pltpu.VMEM((2, rows, depth), jnp.bfloat16),
            block,
            block,
            pltpu.VMEM((WIDE, depth), jnp.bfloat16),
            pltpu.VMEM((2 * rows, depth), jnp.bfloat16),
            pltpu.SemaphoreType.DMA((2,)),
            pltpu.SemaphoreType.DMA((2,)),
            pair,
            pair,
            pair,
            pltpu.SemaphoreType.DMA((2,)),
            pltpu.SemaphoreType.REGULAR,
            pltpu.SemaphoreType.REGULAR,
        ],
        compiler_params=pltpu.CompilerParams(
            collective_id=0, has_side_effects=True, vmem_limit_bytes=40 << 20
        ),
        cost_estimate=pl.CostEstimate(
            flops=22 * rows * rows * depth, bytes_accessed=8 * rows * depth, transcendentals=0
        ),
    )(logit_scale, logit_bias, *inputs)
    return pl.pallas_call(
        finish_kernel,
        out_shape=(
            jax.ShapeDtypeStruct((rows, depth), jnp.bfloat16),
            jax.ShapeDtypeStruct((rows, depth), jnp.bfloat16),
            jax.ShapeDtypeStruct((rows,), jnp.float32),
        ),
        in_specs=[pl.BlockSpec(memory_space=pltpu.VMEM)] * 3,
        out_specs=[pl.BlockSpec(memory_space=pl.ANY)] * 3,
        scratch_shapes=[
            pltpu.VMEM((2, rows, depth), jnp.bfloat16),
            pltpu.VMEM((rows,), jnp.float32),
            pltpu.SemaphoreType.DMA((2, PIECES)),
            pltpu.SemaphoreType.DMA,
        ],
        compiler_params=pltpu.CompilerParams(vmem_limit_bytes=16 << 20),
    )(*totals)


def solution(mesh):
    count = mesh.shape["dp"]
    in_specs = (P("dp", None), P("dp", None), P(), P())
    out_specs = (P("dp", None), P("dp", None), P("dp"))
    return jax.shard_map(
        lambda *arrays: per_device(count, *arrays),
        mesh=mesh,
        in_specs=in_specs,
        out_specs=out_specs,
        check_vma=False,
    )
```

```python
import jax
import jax.numpy as jnp
from jax import lax
from jax.experimental import pallas as pl
from jax.experimental.pallas import tpu as pltpu
from jax.sharding import PartitionSpec as P

MESH = pl.DeviceIdType.MESH
WIDE, NARROW, TAIL = 128, 64, 2
PIECES = 4
PLANE = 128
RELAYS = ((0, 104), (1, 112))
KEEPERS = ((3, 14), (4, 22))
HEAD_START = 1
LOG2E = 1.4426950408889634


def exchange_kernel(
    count,
    scale_ref,
    bias_ref,
    image_ref,
    text_ref,
    total,
    logs,
    lins,
    own,
    early,
    first,
    relayed,
    late,
    own_sem,
    early_sem,
    first_sem,
    second_sem,
    passed_sem,
    relay_sem,
    ready_sem,
    other_sem,
    keeper_sem,
):
    rows, depth = image_ref.shape
    wide = (rows - NARROW * TAIL) // WIDE
    me = lax.axis_index("dp")
    odd = lax.rem(me, 2)
    even = 1 - odd
    other = me + 1 - 2 * odd
    ahead = lax.rem(me + 2, count)
    behind = lax.rem(me + count - 2, count)

    place = lax.rem(me, PLANE)
    is_head = place < 2
    is_tail = place >= PLANE - 2
    even_head = place == 0
    even_tail = place == PLANE - 2
    is_relay = [place == there for _, there in RELAYS]
    is_keeper = [place == there for _, there in KEEPERS]

    def tell(semaphore, device):
        pl.semaphore_signal(semaphore, inc=1, device_id=(device,), device_id_type=MESH)

    barrier = pltpu.get_barrier_semaphore()
    tell(barrier, behind)

    @pl.when(place < PLANE - 4)
    def _():
        tell(barrier, ahead)

    @pl.when(odd == 1)
    def _():
        tell(barrier, other)

    @pl.when(even_head)
    def _():
        for _, there in RELAYS:
            tell(barrier, lax.rem(me - PLANE + there + count, count))

    for chosen, (_, there) in zip(is_relay, RELAYS):

        @pl.when(chosen)
        def _(there=there):
            tell(barrier, me - there + PLANE - 2)

    for chosen, (_, there) in zip(is_keeper, KEEPERS):

        @pl.when(chosen)
        def _(there=there):
            tell(barrier, me - there)
            tell(barrier, lax.rem(me - there - 2 + count, count))

    by_ready = jnp.logical_or(is_head, is_tail)
    heard = 1 + even + jnp.where(by_ready, 0, 1) + jnp.where(even_tail, len(RELAYS), 0)
    heard += sum(jnp.where(chosen, 1, 0) for chosen in is_relay)
    heard += jnp.where(jnp.logical_or(even_head, even_tail), len(KEEPERS), 0)

    loads = []
    for side, ref in ((0, image_ref), (1, text_ref)):
        load = pltpu.make_async_copy(ref, own.at[side], own_sem.at[side])
        load.start()
        loads.append(load)

    def span(index, narrow):
        if narrow:
            start = wide * WIDE + index * NARROW
            return pl.ds(start, NARROW), wide + index
        start = index * WIDE
        if not isinstance(index, int):
            start = pl.multiple_of(start, WIDE)
        return pl.ds(start, WIDE), index

    def send(source, target, sems, where, device, place=None):
        here, index = where
        there = here
        if place is not None:
            there = pl.ds(2 * here.start + place * here.size, here.size)
        return pltpu.make_async_remote_copy(
            src_ref=source.at[here],
            dst_ref=target.at[there],
            send_sem=sems.at[0, index],
            recv_sem=sems.at[1, index],
            device_id=(device,),
            device_id_type=MESH,
        )

    pieces = [span(c, False) for c in range(wide)] + [span(c, True) for c in range(TAIL)]

    def start_all(source, target, sems, device, place=None):
        for where in pieces:
            send(source, target, sems, where, device, place).start()

    def to_relay(piece, there):
        here, index = pieces[piece]
        return pltpu.make_async_remote_copy(
            src_ref=text_ref.at[here],
            dst_ref=relayed.at[pl.ds(0, here.size)],
            send_sem=second_sem.at[0, index],
            recv_sem=relay_sem.at[1],
            device_id=(me - (PLANE - 2) + there,),
            device_id_type=MESH,
        )

    def from_relay(piece, there):
        here, index = pieces[piece]
        return pltpu.make_async_remote_copy(
            src_ref=relayed.at[pl.ds(0, here.size)],
            dst_ref=late.at[pl.ds(2 * here.start, here.size)],
            send_sem=relay_sem.at[0],
            recv_sem=second_sem.at[1, index],
            device_id=(lax.rem(me - there + PLANE, count),),
            device_id_type=MESH,
        )

    def to_keeper(piece, there):
        here, index = pieces[piece]
        return pltpu.make_async_remote_copy(
            src_ref=image_ref.at[here],
            dst_ref=relayed.at[pl.ds(0, here.size)],
            send_sem=first_sem.at[0, index],
            recv_sem=relay_sem.at[1],
            device_id=(me + there,),
            device_id_type=MESH,
        )

    def from_keeper(piece, there):
        here, index = pieces[piece]
        return pltpu.make_async_remote_copy(
            src_ref=relayed.at[pl.ds(0, here.size)],
            dst_ref=first.at[here],
            send_sem=relay_sem.at[0],
            recv_sem=first_sem.at[1, index],
            device_id=(lax.rem(me - there - 2 + count, count),),
            device_id_type=MESH,
        )

    kept = [index for index, _ in KEEPERS]

    def start_unkept():
        for piece, where in enumerate(pieces):
            if piece not in kept:
                send(image_ref, first, first_sem, where, behind).start()

    to_other = pltpu.make_async_remote_copy(
        src_ref=own.at[even],
        dst_ref=early,
        send_sem=early_sem.at[0],
        recv_sem=early_sem.at[1],
        device_id=(other,),
        device_id_type=MESH,
    )

    pl.semaphore_wait(barrier, heard)

    @pl.when(place >= PLANE - 4)
    def _():
        tell(ready_sem, ahead)


    neither = jnp.logical_and(place > 0, place < PLANE - 2)
    early_ready = jnp.logical_not(is_head)

    @pl.when(odd == 1)
    def _():
        start_all(text_ref, first, first_sem, ahead)

    @pl.when(even_head)
    def _():
        for piece, there in KEEPERS:
            to_keeper(piece, there).start()
        start_all(text_ref, late, second_sem, ahead, 0)

    @pl.when(even_tail)
    def _():
        for piece, there in RELAYS:
            to_relay(piece, there).start()
        for _, there in KEEPERS:
            tell(keeper_sem, lax.rem(me + 2 + there, count))

    @pl.when(odd == 0)
    def _():
        tell(other_sem, other)

    total[...] = jnp.zeros_like(total)
    logs[...] = jnp.zeros_like(logs)
    lins[...] = jnp.zeros_like(lins)

    @pl.when(jnp.logical_and(even == 1, early_ready))
    def _():
        @pl.when(is_tail)
        def _():
            pl.semaphore_wait(ready_sem, 1)

        start_all(image_ref, first, first_sem, behind)

    for load in loads:
        load.wait()

    @pl.when(odd == 1)
    def _():
        pl.semaphore_wait(other_sem, 1)

    to_other.start()

    scale = scale_ref[0]
    slope = scale * LOG2E
    shift = bias_ref[0] * LOG2E

    halves = [pl.ds(0, rows // 2), pl.ds(rows // 2, rows // 2)]

    def weigh(side, half, block, base=None):
        logits = (
            lax.dot_general(
                own[side, half], block, (((1,), (1,)), ((), ())), preferred_element_type=jnp.float32
            )
            * slope
            + shift
        )
        small = jnp.exp2(jnp.minimum(logits, -logits))
        below = 1.0 + small
        positive = logits >= 0.0
        linear = jnp.maximum(logits, 0.0)
        if base is None:
            weights = jnp.where(positive, scale, scale * small)
        else:
            row = lax.broadcasted_iota(jnp.int32, logits.shape, 0) + half.start
            column = lax.broadcasted_iota(jnp.int32, logits.shape, 1) + base
            label = row == column
            linear = jnp.where(label, linear - logits, linear)
            weights = jnp.where(
                label,
                jnp.where(positive, -scale * small, -scale),
                jnp.where(positive, scale, scale * small),
            )
        width = min(logits.shape[1], 128)
        for lane in range(0, logits.shape[1], width):
            here = slice(lane, lane + width)
            logs[side, half, :width] = logs[side, half, :width] * below[:, here] + small[:, here]
            lins[side, half, :width] += linear[:, here]
        return (weights * pltpu.reciprocal(below, approx=True)).astype(jnp.bfloat16)

    def add(side, block):
        weights = [weigh(side, half, block) for half in halves]
        for half, factor in zip(halves, weights):
            total[side, half] += jnp.dot(factor, block, preferred_element_type=jnp.float32)

    @pl.loop(0, rows // 256)
    def _(c):
        here = pl.ds(pl.multiple_of(c * 256, 256), 256)
        block = own[1, here]
        weights = [weigh(0, half, block, c * 256) for half in halves]
        for half, factor in zip(halves, weights):
            total[0, half] += jnp.dot(factor, block, preferred_element_type=jnp.float32)
        total[1, here] += sum(
            lax.dot_general(
                factor, own[0, half], (((0,), (0,)), ((), ())), preferred_element_type=jnp.float32
            )
            for half, factor in zip(halves, weights)
        )

    started = jnp.logical_or(odd == 1, early_ready)

    @pl.when(started)
    def _():
        send(own.at[odd], first, first_sem, pieces[0], other).wait_send()

    @pl.when(jnp.logical_and(odd == 1, early_ready))
    def _():
        @pl.when(is_tail)
        def _():
            pl.semaphore_wait(ready_sem, 1)

        start_all(image_ref, late, second_sem, behind, 0)

    @pl.when(jnp.logical_and(even == 1, neither))
    def _():
        start_all(text_ref, late, second_sem, ahead, 0)

    for chosen, (piece, there) in zip(is_relay, RELAYS):

        @pl.when(chosen)
        def _(piece=piece, there=there):
            to_relay(piece, there).wait_recv()
            from_relay(piece, there).start()

    to_other.wait_recv()

    @pl.loop(0, rows // 256)
    def _(c):
        add(even, early[pl.ds(pl.multiple_of(c * 256, 256), 256)])

    @pl.when(even_tail)
    def _():
        for piece, where in enumerate(pieces):
            if piece not in [index for index, _ in RELAYS]:
                send(text_ref, late, second_sem, where, ahead, 0).start()

    def front(index, narrow):
        where = span(index, narrow)
        send(first, first, first_sem, where, other).wait_recv()
        send(first, late, passed_sem, where, other, 1).start()
        add(even, first[where[0]])

    @pl.when(is_head)
    def _():
        pl.semaphore_wait(ready_sem, 1)

        @pl.when(odd == 1)
        def _():
            start_all(image_ref, late, second_sem, behind, 0)

        @pl.when(odd == 0)
        def _():
            @pl.when(me != 0)
            def _():
                start_unkept()

            @pl.loop(0, wide)
            def _(c):
                front(c, False)

                @pl.when(jnp.logical_and(me == 0, c == HEAD_START))
                def _():
                    start_unkept()

            for c in range(TAIL):
                front(c, True)

    def turn(index, narrow):
        where = span(index, narrow)
        here = where[0]

        @pl.when(jnp.logical_not(even_head))
        def _():
            front(index, narrow)

        send(first, late, passed_sem, where, other, 1).wait_recv()
        send(own.at[0], late, second_sem, where, other, 0).wait_recv()
        add(odd, late[pl.ds(2 * here.start, 2 * here.size)])

    @pl.loop(0, wide)
    def _(c):
        turn(c, False)
        for chosen, (piece, there) in zip(is_keeper, KEEPERS):

            @pl.when(jnp.logical_and(chosen, c == 1))
            def _(piece=piece, there=there):
                to_keeper(piece, there).wait_recv()
                pl.semaphore_wait(keeper_sem, 1)
                from_keeper(piece, there).start()

    for c in range(TAIL):
        turn(c, True)

    to_other.wait_send()

    @pl.when(jnp.logical_not(started))
    def _():
        send(own.at[0], first, first_sem, pieces[0], other).wait_send()

    for chosen, (piece, there) in zip(is_relay, RELAYS):

        @pl.when(chosen)
        def _(piece=piece, there=there):
            from_relay(piece, there).wait_send()

    for chosen, (piece, there) in zip(is_keeper, KEEPERS):

        @pl.when(chosen)
        def _(piece=piece, there=there):
            from_keeper(piece, there).wait_send()

    for where in pieces[1:]:
        send(own.at[0], first, first_sem, where, other).wait_send()
    for where in pieces:
        send(own.at[0], late, second_sem, where, other, 0).wait_send()
        send(first, late, passed_sem, where, other, 1).wait_send()


def finish_kernel(total, logs, lins, image_out, text_out, loss_out, held, loss, sems, loss_sem):
    rows = held.shape[1]
    step = rows // PIECES
    copies = []
    for place, out in ((0, image_out), (1, text_out)):
        for c in range(PIECES):
            here = pl.ds(c * step, step)
            held[place, here] = total[place, here].astype(jnp.bfloat16)
            copy = pltpu.make_async_copy(held.at[place, here], out.at[here], sems.at[place, c])
            copy.start()
            copies.append(copy)
    sums = lins[0] * (1.0 / LOG2E) + jnp.log1p(logs[0])
    loss[...] = jnp.sum(sums.T, axis=0) / (3.0 * rows)
    last = pltpu.make_async_copy(loss, loss_out, loss_sem)
    last.start()
    for copy in copies:
        copy.wait()
    last.wait()


def per_device(count, image_emb, text_emb, logit_scale, logit_bias):
    rows, depth = image_emb.shape
    inputs = [pltpu.with_memory_space_constraint(x, pltpu.HBM) for x in (image_emb, text_emb)]
    block = pltpu.VMEM((rows, depth), jnp.bfloat16)
    pieces = (rows - NARROW * TAIL) // WIDE + TAIL
    pair = pltpu.SemaphoreType.DMA((2, pieces))
    totals = pl.pallas_call(
        lambda *refs: exchange_kernel(count, *refs),
        out_shape=(
            pltpu.VMEM((2, rows, depth), jnp.float32),
            pltpu.VMEM((2, rows, 128), jnp.float32),
            pltpu.VMEM((2, rows, 128), jnp.float32),
        ),
        in_specs=[pl.BlockSpec(memory_space=pltpu.SMEM)] * 2
        + [pl.BlockSpec(memory_space=pltpu.HBM)] * 2,
        out_specs=[pl.BlockSpec(memory_space=pltpu.VMEM)] * 3,
        scratch_shapes=[
            pltpu.VMEM((2, rows, depth), jnp.bfloat16),
            block,
            block,
            pltpu.VMEM((WIDE, depth), jnp.bfloat16),
            pltpu.VMEM((2 * rows, depth), jnp.bfloat16),
            pltpu.SemaphoreType.DMA((2,)),
            pltpu.SemaphoreType.DMA((2,)),
            pair,
            pair,
            pair,
            pltpu.SemaphoreType.DMA((2,)),
            pltpu.SemaphoreType.REGULAR,
            pltpu.SemaphoreType.REGULAR,
            pltpu.SemaphoreType.REGULAR,
        ],
        compiler_params=pltpu.CompilerParams(
            collective_id=0, has_side_effects=True, vmem_limit_bytes=40 << 20
        ),
        cost_estimate=pl.CostEstimate(
            flops=22 * rows * rows * depth, bytes_accessed=8 * rows * depth, transcendentals=0
        ),
    )(logit_scale, logit_bias, *inputs)
    return pl.pallas_call(
        finish_kernel,
        out_shape=(
            jax.ShapeDtypeStruct((rows, depth), jnp.bfloat16),
            jax.ShapeDtypeStruct((rows, depth), jnp.bfloat16),
            jax.ShapeDtypeStruct((rows,), jnp.float32),
        ),
        in_specs=[pl.BlockSpec(memory_space=pltpu.VMEM)] * 3,
        out_specs=[pl.BlockSpec(memory_space=pl.ANY)] * 3,
        scratch_shapes=[
            pltpu.VMEM((2, rows, depth), jnp.bfloat16),
            pltpu.VMEM((rows,), jnp.float32),
            pltpu.SemaphoreType.DMA((2, PIECES)),
            pltpu.SemaphoreType.DMA,
        ],
        compiler_params=pltpu.CompilerParams(vmem_limit_bytes=16 << 20),
    )(*totals)


def solution(mesh):
    count = mesh.shape["dp"]
    in_specs = (P("dp", None), P("dp", None), P(), P())
    out_specs = (P("dp", None), P("dp", None), P("dp"))
    return jax.shard_map(
        lambda *arrays: per_device(count, *arrays),
        mesh=mesh,
        in_specs=in_specs,
        out_specs=out_specs,
        check_vma=False,
    )
```

```python
import jax
import jax.numpy as jnp
from jax import lax
from jax.experimental import pallas as pl
from jax.experimental.pallas import tpu as pltpu
from jax.sharding import PartitionSpec as P

MESH = pl.DeviceIdType.MESH
WIDE, NARROW, TAIL = 128, 64, 4
PIECES = 4
PLANE = 128
RELAYS = ((0, 104), (1, 112))
KEEPERS = ((2, 14), (3, 22), (4, 38), (5, 46))
HEAD_START = 1
LOG2E = 1.4426950408889634


def exchange_kernel(
    count,
    scale_ref,
    bias_ref,
    image_ref,
    text_ref,
    total,
    logs,
    lins,
    own,
    early,
    first,
    relayed,
    late,
    own_sem,
    early_sem,
    first_sem,
    second_sem,
    passed_sem,
    relay_sem,
    ready_sem,
    other_sem,
    keeper_sem,
):
    rows, depth = image_ref.shape
    wide = (rows - NARROW * TAIL) // WIDE
    me = lax.axis_index("dp")
    odd = lax.rem(me, 2)
    even = 1 - odd
    other = me + 1 - 2 * odd
    ahead = lax.rem(me + 2, count)
    behind = lax.rem(me + count - 2, count)

    place = lax.rem(me, PLANE)
    is_head = place < 2
    is_tail = place >= PLANE - 2
    even_head = place == 0
    even_tail = place == PLANE - 2
    is_relay = [place == there for _, there in RELAYS]
    is_keeper = [place == there for _, there in KEEPERS]

    def tell(semaphore, device):
        pl.semaphore_signal(semaphore, inc=1, device_id=(device,), device_id_type=MESH)

    barrier = pltpu.get_barrier_semaphore()
    tell(barrier, behind)

    @pl.when(place < PLANE - 4)
    def _():
        tell(barrier, ahead)

    @pl.when(odd == 1)
    def _():
        tell(barrier, other)

    @pl.when(even_head)
    def _():
        for _, there in RELAYS:
            tell(barrier, lax.rem(me - PLANE + there + count, count))

    for chosen, (_, there) in zip(is_relay, RELAYS):

        @pl.when(chosen)
        def _(there=there):
            tell(barrier, me - there + PLANE - 2)

    for chosen, (_, there) in zip(is_keeper, KEEPERS):

        @pl.when(chosen)
        def _(there=there):
            tell(barrier, me - there)
            tell(barrier, lax.rem(me - there - 2 + count, count))

    by_ready = jnp.logical_or(is_head, is_tail)
    heard = 1 + even + jnp.where(by_ready, 0, 1) + jnp.where(even_tail, len(RELAYS), 0)
    heard += sum(jnp.where(chosen, 1, 0) for chosen in is_relay)
    heard += jnp.where(jnp.logical_or(even_head, even_tail), len(KEEPERS), 0)

    loads = []
    for side, ref in ((0, image_ref), (1, text_ref)):
        load = pltpu.make_async_copy(ref, own.at[side], own_sem.at[side])
        load.start()
        loads.append(load)

    def span(index, narrow):
        if narrow:
            start = wide * WIDE + index * NARROW
            return pl.ds(start, NARROW), wide + index
        start = index * WIDE
        if not isinstance(index, int):
            start = pl.multiple_of(start, WIDE)
        return pl.ds(start, WIDE), index

    def send(source, target, sems, where, device, place=None):
        here, index = where
        there = here
        if place is not None:
            there = pl.ds(2 * here.start + place * here.size, here.size)
        return pltpu.make_async_remote_copy(
            src_ref=source.at[here],
            dst_ref=target.at[there],
            send_sem=sems.at[0, index],
            recv_sem=sems.at[1, index],
            device_id=(device,),
            device_id_type=MESH,
        )

    pieces = [span(c, False) for c in range(wide)] + [span(c, True) for c in range(TAIL)]

    def start_all(source, target, sems, device, place=None):
        for where in pieces:
            send(source, target, sems, where, device, place).start()

    def to_relay(piece, there):
        here, index = pieces[piece]
        return pltpu.make_async_remote_copy(
            src_ref=text_ref.at[here],
            dst_ref=relayed.at[pl.ds(0, here.size)],
            send_sem=second_sem.at[0, index],
            recv_sem=relay_sem.at[1],
            device_id=(me - (PLANE - 2) + there,),
            device_id_type=MESH,
        )

    def from_relay(piece, there):
        here, index = pieces[piece]
        return pltpu.make_async_remote_copy(
            src_ref=relayed.at[pl.ds(0, here.size)],
            dst_ref=late.at[pl.ds(2 * here.start, here.size)],
            send_sem=relay_sem.at[0],
            recv_sem=second_sem.at[1, index],
            device_id=(lax.rem(me - there + PLANE, count),),
            device_id_type=MESH,
        )

    def to_keeper(piece, there):
        here, index = pieces[piece]
        return pltpu.make_async_remote_copy(
            src_ref=image_ref.at[here],
            dst_ref=relayed.at[pl.ds(0, here.size)],
            send_sem=first_sem.at[0, index],
            recv_sem=relay_sem.at[1],
            device_id=(me + there,),
            device_id_type=MESH,
        )

    def from_keeper(piece, there):
        here, index = pieces[piece]
        return pltpu.make_async_remote_copy(
            src_ref=relayed.at[pl.ds(0, here.size)],
            dst_ref=first.at[here],
            send_sem=relay_sem.at[0],
            recv_sem=first_sem.at[1, index],
            device_id=(lax.rem(me - there - 2 + count, count),),
            device_id_type=MESH,
        )

    kept = [index for index, _ in KEEPERS]

    def start_unkept():
        for piece, where in enumerate(pieces):
            if piece not in kept:
                send(image_ref, first, first_sem, where, behind).start()

    to_other = pltpu.make_async_remote_copy(
        src_ref=own.at[even],
        dst_ref=early,
        send_sem=early_sem.at[0],
        recv_sem=early_sem.at[1],
        device_id=(other,),
        device_id_type=MESH,
    )

    pl.semaphore_wait(barrier, heard)

    @pl.when(place >= PLANE - 4)
    def _():
        tell(ready_sem, ahead)


    neither = jnp.logical_and(place > 0, place < PLANE - 2)
    early_ready = jnp.logical_not(is_head)

    @pl.when(odd == 1)
    def _():
        start_all(text_ref, first, first_sem, ahead)

    @pl.when(even_head)
    def _():
        for piece, there in KEEPERS:
            to_keeper(piece, there).start()
        start_all(text_ref, late, second_sem, ahead, 0)

    @pl.when(even_tail)
    def _():
        for piece, there in RELAYS:
            to_relay(piece, there).start()
        for _, there in KEEPERS:
            tell(keeper_sem, lax.rem(me + 2 + there, count))

    @pl.when(odd == 0)
    def _():
        tell(other_sem, other)

    total[...] = jnp.zeros_like(total)
    logs[...] = jnp.zeros_like(logs)
    lins[...] = jnp.zeros_like(lins)

    @pl.when(jnp.logical_and(even == 1, early_ready))
    def _():
        @pl.when(is_tail)
        def _():
            pl.semaphore_wait(ready_sem, 1)

        start_all(image_ref, first, first_sem, behind)

    for load in loads:
        load.wait()

    @pl.when(odd == 1)
    def _():
        pl.semaphore_wait(other_sem, 1)

    to_other.start()

    scale = scale_ref[0]
    slope = scale * LOG2E
    shift = bias_ref[0] * LOG2E

    halves = [pl.ds(0, rows // 2), pl.ds(rows // 2, rows // 2)]

    def weigh(side, half, block, base=None):
        logits = (
            lax.dot_general(
                own[side, half], block, (((1,), (1,)), ((), ())), preferred_element_type=jnp.float32
            )
            * slope
            + shift
        )
        small = jnp.exp2(jnp.minimum(logits, -logits))
        below = 1.0 + small
        positive = logits >= 0.0
        linear = jnp.maximum(logits, 0.0)
        if base is None:
            weights = jnp.where(positive, scale, scale * small)
        else:
            row = lax.broadcasted_iota(jnp.int32, logits.shape, 0) + half.start
            column = lax.broadcasted_iota(jnp.int32, logits.shape, 1) + base
            label = row == column
            linear = jnp.where(label, linear - logits, linear)
            weights = jnp.where(
                label,
                jnp.where(positive, -scale * small, -scale),
                jnp.where(positive, scale, scale * small),
            )
        width = min(logits.shape[1], 128)
        for lane in range(0, logits.shape[1], width):
            here = slice(lane, lane + width)
            logs[side, half, :width] = logs[side, half, :width] * below[:, here] + small[:, here]
            lins[side, half, :width] += linear[:, here]
        return (weights * pltpu.reciprocal(below, approx=True)).astype(jnp.bfloat16)

    def add(side, block):
        weights = [weigh(side, half, block) for half in halves]
        for half, factor in zip(halves, weights):
            total[side, half] += jnp.dot(factor, block, preferred_element_type=jnp.float32)

    @pl.loop(0, rows // 256)
    def _(c):
        here = pl.ds(pl.multiple_of(c * 256, 256), 256)
        block = own[1, here]
        weights = [weigh(0, half, block, c * 256) for half in halves]
        for half, factor in zip(halves, weights):
            total[0, half] += jnp.dot(factor, block, preferred_element_type=jnp.float32)
        total[1, here] += sum(
            lax.dot_general(
                factor, own[0, half], (((0,), (0,)), ((), ())), preferred_element_type=jnp.float32
            )
            for half, factor in zip(halves, weights)
        )

    started = jnp.logical_or(odd == 1, early_ready)

    @pl.when(started)
    def _():
        send(own.at[odd], first, first_sem, pieces[0], other).wait_send()

    @pl.when(jnp.logical_and(odd == 1, early_ready))
    def _():
        @pl.when(is_tail)
        def _():
            pl.semaphore_wait(ready_sem, 1)

        start_all(image_ref, late, second_sem, behind, 0)

    @pl.when(jnp.logical_and(even == 1, neither))
    def _():
        start_all(text_ref, late, second_sem, ahead, 0)

    for chosen, (piece, there) in zip(is_relay, RELAYS):

        @pl.when(chosen)
        def _(piece=piece, there=there):
            to_relay(piece, there).wait_recv()
            from_relay(piece, there).start()

    to_other.wait_recv()

    @pl.loop(0, rows // 256)
    def _(c):
        add(even, early[pl.ds(pl.multiple_of(c * 256, 256), 256)])

    @pl.when(even_tail)
    def _():
        for piece, where in enumerate(pieces):
            if piece not in [index for index, _ in RELAYS]:
                send(text_ref, late, second_sem, where, ahead, 0).start()

    def front(index, narrow):
        where = span(index, narrow)
        send(first, first, first_sem, where, other).wait_recv()
        send(first, late, passed_sem, where, other, 1).start()
        add(even, first[where[0]])

    @pl.when(is_head)
    def _():
        pl.semaphore_wait(ready_sem, 1)

        @pl.when(odd == 1)
        def _():
            start_all(image_ref, late, second_sem, behind, 0)

        @pl.when(odd == 0)
        def _():
            @pl.when(me != 0)
            def _():
                start_unkept()

            @pl.loop(0, wide)
            def _(c):
                front(c, False)

                @pl.when(jnp.logical_and(me == 0, c == HEAD_START))
                def _():
                    start_unkept()

            for c in range(TAIL):
                front(c, True)

    def turn(index, narrow):
        where = span(index, narrow)
        here = where[0]

        @pl.when(jnp.logical_not(even_head))
        def _():
            front(index, narrow)

        send(first, late, passed_sem, where, other, 1).wait_recv()
        send(own.at[0], late, second_sem, where, other, 0).wait_recv()
        add(odd, late[pl.ds(2 * here.start, 2 * here.size)])

    @pl.loop(0, wide)
    def _(c):
        turn(c, False)
        for chosen, (piece, there) in zip(is_keeper, KEEPERS):

            @pl.when(jnp.logical_and(chosen, c == 1))
            def _(piece=piece, there=there):
                to_keeper(piece, there).wait_recv()
                pl.semaphore_wait(keeper_sem, 1)
                from_keeper(piece, there).start()

    for c in range(TAIL):
        turn(c, True)

    to_other.wait_send()

    @pl.when(jnp.logical_not(started))
    def _():
        send(own.at[0], first, first_sem, pieces[0], other).wait_send()

    for chosen, (piece, there) in zip(is_relay, RELAYS):

        @pl.when(chosen)
        def _(piece=piece, there=there):
            from_relay(piece, there).wait_send()

    for chosen, (piece, there) in zip(is_keeper, KEEPERS):

        @pl.when(chosen)
        def _(piece=piece, there=there):
            from_keeper(piece, there).wait_send()

    for where in pieces[1:]:
        send(own.at[0], first, first_sem, where, other).wait_send()
    for where in pieces:
        send(own.at[0], late, second_sem, where, other, 0).wait_send()
        send(first, late, passed_sem, where, other, 1).wait_send()


def finish_kernel(total, logs, lins, image_out, text_out, loss_out, held, loss, sems, loss_sem):
    rows = held.shape[1]
    step = rows // PIECES
    copies = []
    for place, out in ((0, image_out), (1, text_out)):
        for c in range(PIECES):
            here = pl.ds(c * step, step)
            held[place, here] = total[place, here].astype(jnp.bfloat16)
            copy = pltpu.make_async_copy(held.at[place, here], out.at[here], sems.at[place, c])
            copy.start()
            copies.append(copy)
    sums = lins[0] * (1.0 / LOG2E) + jnp.log1p(logs[0])
    loss[...] = jnp.sum(sums.T, axis=0) / (3.0 * rows)
    last = pltpu.make_async_copy(loss, loss_out, loss_sem)
    last.start()
    for copy in copies:
        copy.wait()
    last.wait()


def per_device(count, image_emb, text_emb, logit_scale, logit_bias):
    rows, depth = image_emb.shape
    inputs = [pltpu.with_memory_space_constraint(x, pltpu.HBM) for x in (image_emb, text_emb)]
    block = pltpu.VMEM((rows, depth), jnp.bfloat16)
    pieces = (rows - NARROW * TAIL) // WIDE + TAIL
    pair = pltpu.SemaphoreType.DMA((2, pieces))
    totals = pl.pallas_call(
        lambda *refs: exchange_kernel(count, *refs),
        out_shape=(
            pltpu.VMEM((2, rows, depth), jnp.float32),
            pltpu.VMEM((2, rows, 128), jnp.float32),
            pltpu.VMEM((2, rows, 128), jnp.float32),
        ),
        in_specs=[pl.BlockSpec(memory_space=pltpu.SMEM)] * 2
        + [pl.BlockSpec(memory_space=pltpu.HBM)] * 2,
        out_specs=[pl.BlockSpec(memory_space=pltpu.VMEM)] * 3,
        scratch_shapes=[
            pltpu.VMEM((2, rows, depth), jnp.bfloat16),
            block,
            block,
            pltpu.VMEM((WIDE, depth), jnp.bfloat16),
            pltpu.VMEM((2 * rows, depth), jnp.bfloat16),
            pltpu.SemaphoreType.DMA((2,)),
            pltpu.SemaphoreType.DMA((2,)),
            pair,
            pair,
            pair,
            pltpu.SemaphoreType.DMA((2,)),
            pltpu.SemaphoreType.REGULAR,
            pltpu.SemaphoreType.REGULAR,
            pltpu.SemaphoreType.REGULAR,
        ],
        compiler_params=pltpu.CompilerParams(
            collective_id=0, has_side_effects=True, vmem_limit_bytes=40 << 20
        ),
        cost_estimate=pl.CostEstimate(
            flops=22 * rows * rows * depth, bytes_accessed=8 * rows * depth, transcendentals=0
        ),
    )(logit_scale, logit_bias, *inputs)
    return pl.pallas_call(
        finish_kernel,
        out_shape=(
            jax.ShapeDtypeStruct((rows, depth), jnp.bfloat16),
            jax.ShapeDtypeStruct((rows, depth), jnp.bfloat16),
            jax.ShapeDtypeStruct((rows,), jnp.float32),
        ),
        in_specs=[pl.BlockSpec(memory_space=pltpu.VMEM)] * 3,
        out_specs=[pl.BlockSpec(memory_space=pl.ANY)] * 3,
        scratch_shapes=[
            pltpu.VMEM((2, rows, depth), jnp.bfloat16),
            pltpu.VMEM((rows,), jnp.float32),
            pltpu.SemaphoreType.DMA((2, PIECES)),
            pltpu.SemaphoreType.DMA,
        ],
        compiler_params=pltpu.CompilerParams(vmem_limit_bytes=16 << 20),
    )(*totals)


def solution(mesh):
    count = mesh.shape["dp"]
    in_specs = (P("dp", None), P("dp", None), P(), P())
    out_specs = (P("dp", None), P("dp", None), P("dp"))
    return jax.shard_map(
        lambda *arrays: per_device(count, *arrays),
        mesh=mesh,
        in_specs=in_specs,
        out_specs=out_specs,
        check_vma=False,
    )
```
